512 devices in a mesh: depth: 4 (over z_hi, core), row: 16 (over x, y), col: 8 (over z_lo).
Axes of the slice: x: 4, y: 4, z: 16 (z_hi: 2, z_lo: 8; z = z_hi * 8 + z_lo), core: 2. Of those that a mesh axis runs over, the one named last changes fastest.
Arguments:
- gate: bfloat16 [4096, 14336], P(('depth', 'col'), 'row'), may hold values from -6 to 6
- up: bfloat16 [4096, 14336], P(('depth', 'col'), 'row'), may hold values from -6 to 6
- down_weight: bfloat16 [14336, 8192], P('row', 'col'), may hold values from -0.046875 to 0.046875
- cotangent: bfloat16 [4096, 8192], P(('depth', 'row'), 'col'), may hold values from -6 to 6
Outputs:
- output: bfloat16 [4096, 8192], P(('depth', 'row'), 'col')
- grad_gate: bfloat16 [4096, 14336], P(('depth', 'col'), 'row')
- grad_up: bfloat16 [4096, 14336], P(('depth', 'col'), 'row')
- grad_weight: bfloat16 [14336, 8192], P('row', 'col')
The draws below stay inside these ranges and needn't reach their ends.
All inputs are finite; a program needn't handle non-finite values.
Results may differ from the reference program's by a relative error of at most 0.022.
Values may be sent and summed in bfloat16 or wider, within the bound.
No kernel may reach another device: no remote copies, remote signals or barrier semaphores. Data moves between devices by JAX's collectives and lax.ppermute only.
A program may use at most 64 MiB of HBM per device.

```python
import jax
import jax.numpy as jnp
from jax import lax

D = 8192
FF = 14336
TOKENS = 4096
N_DEPTH = 4
N_ROW = 16
N_COL = 8


def block_levels(key, shape, shards, least, top_value):
    def one(position, parts):
        draws = jax.random.uniform(jax.random.fold_in(jax.random.fold_in(key, 6), position), (parts,), jnp.float32, least / len(shards), top_value / len(shards))
        return jnp.repeat(jnp.exp(draws), shape[position] // parts).reshape((-1,) + (1,) * (len(shape) - position - 1))

    gain = one(*shards[0])
    for cut in shards[1:]:
        gain = gain * one(*cut)
    return gain


def bell_draw(rng, dims, spread, bound, pieces=(), kind=jnp.bfloat16):
    result = jax.random.normal(rng, dims, jnp.float32) * spread
    if len(pieces) > 0:
        result = block_levels(rng, dims, pieces, -0.22, 0.18) * result
    return jnp.clip(result, min=-bound, max=bound).astype(kind)


def setup_inputs(seed: int = 0) -> dict:
    key_of = jax.random.split(jax.random.key(seed), 5)
    gate = bell_draw(key_of[0], (TOKENS, FF), 1.0, 6.0, ((0, 32), (1, 16)))
    up = bell_draw(key_of[1], (TOKENS, FF), 1.0, 6.0, ((0, 32), (1, 16)))
    down_weight = bell_draw(key_of[2], (FF, D), FF ** -0.5, 0.046875, ((0, 16), (1, 8)))
    cotangent = bell_draw(key_of[3], (TOKENS, D), 1.0, 6.0, ((0, 64), (1, 8)))
    return {"gate": gate, "up": up, "down_weight": down_weight, "cotangent": cotangent}


def reference(gate, up, down_weight, cotangent):
    gate_f = gate.astype(jnp.float32)
    up_f = up.astype(jnp.float32)
    sig = jax.nn.sigmoid(gate_f)
    silu_v = gate_f * sig
    hidden = (silu_v * up_f).astype(jnp.bfloat16)
    hid_blocks = hidden.reshape(TOKENS, N_ROW, FF // N_ROW).transpose(1, 0, 2)
    wrow_blocks = down_weight.reshape(N_ROW, FF // N_ROW, D)

    def fwd_step(total, pair):
        term = jnp.dot(pair[0], pair[1], preferred_element_type=jnp.float32)
        return total + term.astype(jnp.bfloat16).astype(jnp.float32), None

    output_sum, _ = lax.scan(fwd_step, jnp.zeros((TOKENS, D), jnp.float32), (hid_blocks, wrow_blocks))
    output = output_sum.astype(jnp.bfloat16)

    cot_blocks = cotangent.reshape(TOKENS, N_COL, D // N_COL).transpose(1, 0, 2)
    wcol_blocks = down_weight.reshape(FF, N_COL, D // N_COL).transpose(1, 0, 2)

    def bwd_step(total, pair):
        term = lax.dot_general(pair[0], pair[1], (((1,), (1,)), ((), ())), preferred_element_type=jnp.float32)
        return total + term.astype(jnp.bfloat16).astype(jnp.float32), None

    grad_hidden, _ = lax.scan(bwd_step, jnp.zeros((TOKENS, FF), jnp.float32), (cot_blocks, wcol_blocks))
    grad_gate = (grad_hidden * up_f * sig * (1.0 + gate_f * (1.0 - sig))).astype(jnp.bfloat16)
    grad_up = (grad_hidden * silu_v).astype(jnp.bfloat16)

    hid_planes = hidden.reshape(N_DEPTH, TOKENS // N_DEPTH, FF)
    cot_planes = cotangent.reshape(N_DEPTH, TOKENS // N_DEPTH, D)

    def plane_step(total, pair):
        term = lax.dot_general(pair[0], pair[1], (((0,), (0,)), ((), ())), preferred_element_type=jnp.float32)
        return total + term.astype(jnp.bfloat16).astype(jnp.float32), None

    weight_sum, _ = lax.scan(plane_step, jnp.zeros((FF, D), jnp.float32), (hid_planes, cot_planes))
    grad_weight = weight_sum.astype(jnp.bfloat16)
    return output, grad_gate, grad_up, grad_weight
```

```python
import functools

import jax
import jax.numpy as jnp
from jax import lax
from jax.experimental import pallas as pl
from jax.experimental.pallas import tpu as pltpu
from jax.sharding import Mesh
from jax.sharding import PartitionSpec as P

BF, F32 = jnp.bfloat16, jnp.float32
AXES = ("zhi", "core", "x", "y", "col")
DIMS = (2, 2, 4, 4, 8)
RING = ("zhi", "col")
VMEM_LIMIT = 40 * 2**20


def flat(c):
    n = 0
    for v, d in zip(c, DIMS):
        n = n * d + v % d
    return n


def pairs(move):
    out = []
    for h in range(2):
        for k in range(2):
            for x in range(4):
                for y in range(4):
                    for c in range(8):
                        out.append((flat((h, k, x, y, c)), flat(move(h, k, x, y, c))))
    return out


def ring_move(s):
    def move(h, k, x, y, c):
        z = (h * 8 + c + s) % 16
        return (z // 8, k, x, y, z % 8)

    return pairs(move)


def plane_move(first, s):
    def move(h, k, x, y, c):
        if (k == 0) == first:
            return (h, k, x + s, y, c)
        return (h, k, x, y + s, c)

    return pairs(move)


SWAP_Z = pairs(lambda h, k, x, y, c: (1 - h, k, x, y, c))
SWAP_CORE = pairs(lambda h, k, x, y, c: (h, 1 - k, x, y, c))


def send(a, perm):
    return lax.ppermute(a, AXES, perm)


def place(pos_ref):
    return pos_ref[0], pos_ref[1], pos_ref[2], pos_ref[3], pos_ref[4]


def cot_rows(cots, pos, zh, x, y):
    h0, core, x0, y0, _ = pos
    kx, ky = (x - x0 + 4) % 4, (y - y0 + 4) % 4
    k1 = jnp.where(core == 0, kx, ky)
    k2 = jnp.where(core == 0, ky, kx)
    zr = (zh + h0) % 2
    return cots[k2, k1, zr]


def term_kernel(pos_ref, cot_ref, w_ref, *out_refs):
    pos = place(pos_ref)
    z = pos[0] * 8 + pos[4]

    def rows(k, halves):
        t = (z + k + 16) % 16
        tl = t % 8
        return [cot_rows(cot_ref, pos, t // 8, tl // 2, (tl % 2) * 2 + h) for h in halves]

    def dot(a):
        return lax.dot_general(
            a, w_ref[...], (((1,), (1,)), ((), ())), preferred_element_type=F32
        ).astype(BF)

    r = dot(jnp.concatenate(rows(4, (0,)) + rows(-4, (1,)) + rows(3, (0, 1)), axis=0))
    out_refs[0][...] = r[:64]
    out_refs[1][...] = r[64:128]
    out_refs[2][...] = r[128:]
    for n, (k, l) in enumerate(((-3, 2), (-2, 1), (-1, 0))):
        r = dot(jnp.concatenate(rows(k, (0, 1)) + rows(l, (0, 1)), axis=0))
        out_refs[3 + 2 * n][...] = r[:128]
        out_refs[4 + 2 * n][...] = r[128:]


def out_kernel(pos_ref, hid_ref, w_ref, *out_refs):
    h0, core, x0, y0, _ = place(pos_ref)
    for j in range(4):
        parts = []
        for i in range(4):
            dx = jnp.where(core == 0, j, i)
            dy = jnp.where(core == 0, i, j)
            row = ((x0 + dx) % 4) * 4 + (y0 + dy) % 4
            parts.append(hid_ref[h0 * 16 + row])
        out_refs[j][...] = jnp.dot(
            jnp.concatenate(parts, axis=0), w_ref[...], preferred_element_type=F32
        ).astype(BF)


def grad_kernel(pos_ref, hid_ref, cot_ref, out_ref, flat_ref):
    pos = place(pos_ref)

    @pl.when(pl.program_id(0) == 0)
    def _():
        for zh in range(2):
            for x in range(4):
                for y in range(4):
                    at = ((zh * 4 + x) * 4 + y) * 64
                    flat_ref[at : at + 64, :] = cot_rows(cot_ref, pos, zh, x, y)

    n = pl.multiple_of(pl.program_id(0) * 256, 256)
    out_ref[...] = lax.dot_general(
        hid_ref[...], flat_ref[:, pl.ds(n, 256)], (((0,), (0,)), ((), ())), preferred_element_type=F32
    ).astype(BF)


SMEM = pl.BlockSpec(memory_space=pltpu.SMEM)
VMEM = pl.BlockSpec(memory_space=pltpu.VMEM)
PARAMS = pltpu.CompilerParams(vmem_limit_bytes=VMEM_LIMIT)


def terms_of(pos, cots, w):
    rows = (64, 64) + (128,) * 7
    return pl.pallas_call(
        term_kernel,
        out_shape=[jax.ShapeDtypeStruct((n, 896), BF) for n in rows],
        in_specs=[SMEM, VMEM, VMEM],
        out_specs=[VMEM] * 9,
        compiler_params=PARAMS,
        cost_estimate=pl.CostEstimate(flops=2 * 1024 * 896 * 1024, bytes_accessed=8 * 2**20, transcendentals=0),
        name="hidden_terms",
    )(pos, cots, w)


def out_of(pos, hid, w):
    return pl.pallas_call(
        out_kernel,
        out_shape=[jax.ShapeDtypeStruct((256, 1024), BF)] * 4,
        in_specs=[SMEM, VMEM, VMEM],
        out_specs=[VMEM] * 4,
        compiler_params=PARAMS,
        cost_estimate=pl.CostEstimate(flops=2 * 1024 * 896 * 1024, bytes_accessed=8 * 2**20, transcendentals=0),
        name="output_terms",
    )(pos, hid.reshape(32, 64, 896), w)


def grad_of(pos, hid, cots):
    return pl.pallas_call(
        grad_kernel,
        grid=(4,),
        out_shape=jax.ShapeDtypeStruct((896, 1024), BF),
        in_specs=[SMEM, VMEM, VMEM],
        out_specs=pl.BlockSpec((896, 256), lambda n: (0, n)),
        scratch_shapes=[pltpu.VMEM((2048, 1024), BF)],
        compiler_params=PARAMS,
        cost_estimate=pl.CostEstimate(flops=2 * 2048 * 896 * 1024, bytes_accessed=10 * 2**20, transcendentals=0),
        name="weight_terms",
    )(pos, hid, cots)


def gather_step(a, first):
    return [a, send(a, plane_move(first, -1)), send(a, plane_move(first, 2)), send(a, plane_move(first, 1))]


def per_device(gate, up, w, cot):
    pos = jnp.stack([lax.axis_index(a) for a in AXES]).astype(jnp.int32)
    gate_f, up_f = gate.astype(F32), up.astype(F32)
    sig = jax.nn.sigmoid(gate_f)
    silu_v = gate_f * sig
    hidden = lax.optimization_barrier((silu_v * up_f).astype(BF))
    hid_all = lax.all_gather(hidden, RING, axis=0, tiled=True)

    both = jnp.stack([cot, send(cot, SWAP_Z)])
    line = jnp.stack(gather_step(both, True))
    cots = jnp.stack(gather_step(line, False))

    terms = terms_of(pos, cots, w)
    p4, m4, p3, m3, p2, m2, p1, m1, own = terms[0], terms[1], terms[2], terms[3], terms[4], terms[5], terms[6], terms[7], terms[8]
    right, left = ring_move(1), ring_move(-1)
    a, b = send(p4, right), send(m4, left)
    a = jnp.concatenate([(p3[:64].astype(F32) + a.astype(F32)).astype(BF), p3[64:]], axis=0)
    b = jnp.concatenate([m3[:64], (m3[64:].astype(F32) + b.astype(F32)).astype(BF)], axis=0)
    a, b = send(a, right), send(b, left)
    for p, m in ((p2, m2), (p1, m1)):
        a = send((a.astype(F32) + p.astype(F32)).astype(BF), right)
        b = send((b.astype(F32) + m.astype(F32)).astype(BF), left)
    grad_hidden = own.astype(F32) + a.astype(F32) + b.astype(F32)
    grad_gate = (grad_hidden * up_f * sig * (1.0 + gate_f * (1.0 - sig))).astype(BF)
    grad_up = (grad_hidden * silu_v).astype(BF)

    o = out_of(pos, hid_all, w)
    got = (o[0], send(o[1], plane_move(True, 1)), send(o[2], plane_move(True, 2)), send(o[3], plane_move(True, -1)))

    def piece(i):
        s = slice(64 * i, 64 * i + 64)
        return sum(g[s].astype(F32) for g in got)

    got2 = [send(piece(i).astype(BF), plane_move(False, s)) for i, s in ((1, 1), (2, 2), (3, -1))]
    output = (piece(0) + sum(g.astype(F32) for g in got2)).astype(BF)

    mine = grad_of(pos, hid_all, cots)
    other = send(mine, SWAP_CORE)
    grad_weight = (mine.astype(F32) + other.astype(F32)).astype(BF)
    return output, grad_gate, grad_up, grad_weight


def solution(mesh):
    mesh = Mesh(mesh.devices.reshape(DIMS), AXES)
    depth, row = ("zhi", "core"), ("x", "y")
    by_col, by_row = P(depth + ("col",), row), P(depth + row, "col")
    weight = P(row, "col")
    return jax.shard_map(
        per_device,
        mesh=mesh,
        in_specs=(by_col, by_col, weight, by_row),
        out_specs=(by_row, by_col, by_col, weight),
        check_vma=False,
    )
```

```python
import functools

import jax
import jax.numpy as jnp
from jax import lax
from jax.experimental import pallas as pl
from jax.experimental.pallas import tpu as pltpu
from jax.sharding import Mesh
from jax.sharding import PartitionSpec as P

BF, F32 = jnp.bfloat16, jnp.float32
AXES = ("zhi", "core", "x", "y", "col")
DIMS = (2, 2, 4, 4, 8)
RING = ("zhi", "col")
PLANE = ("x", "y")
VMEM_LIMIT = 20 * 2**20


def flat(c):
    n = 0
    for v, d in zip(c, DIMS):
        n = n * d + v % d
    return n


def pairs(move):
    out = []
    for h in range(2):
        for k in range(2):
            for x in range(4):
                for y in range(4):
                    for c in range(8):
                        out.append((flat((h, k, x, y, c)), flat(move(h, k, x, y, c))))
    return out


def ring_move(s):
    def move(h, k, x, y, c):
        z = (h * 8 + c + s) % 16
        return (z // 8, k, x, y, z % 8)

    return pairs(move)


def half_of(h0, col, row):
    k = (row // 2 - col + 11) % 8 - 3
    return (h0 * 8 + col + k + 16) % 16 // 8


def swap_z(wanted):
    out = []
    for h in range(2):
        for k in range(2):
            for x in range(4):
                for y in range(4):
                    for c in range(8):
                        if (half_of(h, c, x * 4 + y) == h) == wanted:
                            out.append((flat((h, k, x, y, c)), flat((1 - h, k, x, y, c))))
    return out


SWAP_CORE = pairs(lambda h, k, x, y, c: (h, 1 - k, x, y, c))
SMEM = pl.BlockSpec(memory_space=pltpu.SMEM)
VMEM = pl.BlockSpec(memory_space=pltpu.VMEM)
ANY = pl.BlockSpec(memory_space=pl.ANY)
PARAMS = pltpu.CompilerParams(vmem_limit_bytes=VMEM_LIMIT)


def cost(flops, mib):
    return pl.CostEstimate(flops=flops, bytes_accessed=int(mib * 2**20), transcendentals=0)


def send(a, perm):
    return lax.ppermute(a, AXES, perm)


def hidden_kernel(gate_ref, up_ref, out_ref):
    g = gate_ref[...].astype(F32)
    out_ref[...] = (g * jax.nn.sigmoid(g) * up_ref[...].astype(F32)).astype(BF)


def hidden_of(gate, up):
    return pl.pallas_call(
        hidden_kernel,
        out_shape=jax.ShapeDtypeStruct(gate.shape, BF),
        grid=(4,),
        in_specs=[pl.BlockSpec((32, 896), lambda i: (i, 0))] * 2,
        out_specs=pl.BlockSpec((32, 896), lambda i: (i, 0)),
        compiler_params=PARAMS,
        cost_estimate=cost(2**20, 1),
        name="hidden",
    )(gate, up)


def copies_kernel(far_wanted, pos_ref, cot_ref, far_ref, *refs):
    mine = half_of(pos_ref[0], pos_ref[4], pos_ref[2] * 4 + pos_ref[3]) == pos_ref[0]

    def fill(ref):
        for i in range(16):
            refs[-1][i] = ref[...]

    pl.when(mine if far_wanted else jnp.logical_not(mine))(lambda: fill(far_ref))
    pl.when(jnp.logical_not(mine) if far_wanted else mine)(lambda: fill(cot_ref))


def copies_of(pos, cot, far_wanted, *after):
    return pl.pallas_call(
        functools.partial(copies_kernel, far_wanted),
        out_shape=jax.ShapeDtypeStruct((16, 64, 1024), BF),
        in_specs=[SMEM, VMEM, VMEM] + [ANY] * len(after),
        out_specs=VMEM,
        compiler_params=PARAMS,
        cost_estimate=cost(0, 2),
        name="copies",
    )(pos, cot, send(cot, swap_z(far_wanted)), *after)


def exchange(blocks):
    return lax.all_to_all(blocks, PLANE, 0, 0, tiled=True)


def term_kernel(pos_ref, near_ref, w_ref, *refs):
    p43, m32, p2, p1, m1, here = refs[-6:]
    col = pos_ref[4]

    def dot(k, l):
        a = jnp.concatenate([near_ref[(col + k + 8) % 8], near_ref[(col + l + 8) % 8]], axis=0)
        return lax.dot_general(
            a, w_ref[...], (((1,), (1,)), ((), ())), preferred_element_type=F32
        ).astype(BF)

    p43[...] = dot(4, 3)
    m32[...] = dot(-3, -2)
    r = dot(2, 1)
    p2[...] = r[:128]
    p1[...] = r[128:]
    r = dot(-1, 0)
    m1[...] = r[:128]
    here[...] = r[128:]


def terms_of(pos, near, w, *after):
    return pl.pallas_call(
        term_kernel,
        out_shape=[jax.ShapeDtypeStruct((n, 896), BF) for n in (256, 256, 128, 128, 128, 128)],
        in_specs=[SMEM, VMEM, VMEM] + [ANY] * len(after),
        out_specs=[VMEM] * 6,
        compiler_params=PARAMS,
        cost_estimate=cost(2 * 1024 * 896 * 1024, 8),
        name="hidden_terms",
    )(pos, near.reshape(8, 128, 1024), w, *after)


def out_kernel(pos_ref, hid_ref, w_ref, out_ref):
    at = pos_ref[0] * 1024
    for i in range(4):
        a = hid_ref[pl.ds(pl.multiple_of(at + 256 * i, 256), 256), :]
        out_ref[256 * i : 256 * i + 256] = jnp.dot(a, w_ref[...], preferred_element_type=F32).astype(BF)


def out_of(pos, hid, w):
    return pl.pallas_call(
        out_kernel,
        out_shape=jax.ShapeDtypeStruct((1024, 1024), BF),
        in_specs=[SMEM, VMEM, VMEM],
        out_specs=VMEM,
        compiler_params=PARAMS,
        cost_estimate=cost(2 * 1024 * 896 * 1024, 8),
        name="output_terms",
    )(pos, hid, w)


def total_kernel(got_ref, out_ref):
    total = got_ref[0].astype(F32)
    for i in range(1, 16):
        total = total + got_ref[i].astype(F32)
    out_ref[...] = total.astype(BF)


def total_of(got):
    return pl.pallas_call(
        total_kernel,
        grid=(4,),
        out_shape=jax.ShapeDtypeStruct((64, 1024), BF),
        in_specs=[pl.BlockSpec((16, 16, 1024), lambda i: (0, i, 0))],
        out_specs=pl.BlockSpec((16, 1024), lambda i: (i, 0)),
        compiler_params=PARAMS,
        cost_estimate=cost(2**20, 2),
        name="output_sum",
    )(got)


def grad_kernel(pos_ref, hid_ref, near_ref, rest_ref, *refs):
    out_ref, cot_ref = refs[-2:]
    h0, col = pos_ref[0], pos_ref[4]

    @pl.when(pl.program_id(0) == 0)
    def _():
        for r in range(16):
            h = half_of(h0, col, r)
            cot_ref[pl.ds(pl.multiple_of(h * 1024 + r * 64, 64), 64), :] = near_ref[r]
            cot_ref[pl.ds(pl.multiple_of((1 - h) * 1024 + r * 64, 64), 64), :] = rest_ref[r]

    n = pl.multiple_of(pl.program_id(0) * 256, 256)
    out_ref[...] = lax.dot_general(
        hid_ref[...], cot_ref[:, pl.ds(n, 256)], (((0,), (0,)), ((), ())), preferred_element_type=F32
    ).astype(BF)


def grad_of(pos, hid, near, rest, *after):
    return pl.pallas_call(
        grad_kernel,
        grid=(4,),
        out_shape=jax.ShapeDtypeStruct((896, 1024), BF),
        in_specs=[SMEM, VMEM, VMEM, VMEM] + [ANY] * len(after),
        out_specs=pl.BlockSpec((896, 256), lambda n: (0, n)),
        scratch_shapes=[pltpu.VMEM((2048, 1024), BF)],
        compiler_params=PARAMS,
        cost_estimate=cost(2 * 2048 * 896 * 1024, 10),
        name="weight_terms",
    )(pos, hid, near, rest, *after)


def add(a, b):
    return (a.astype(F32) + b.astype(F32)).astype(BF)


def sum_kernel(a_ref, b_ref, p2_ref, p1_ref, m1_ref, *refs):
    c, d, e = refs[-3:]
    c[...] = (a_ref[:128].astype(F32) + p2_ref[...].astype(F32)).astype(BF)
    d[...] = (a_ref[128:].astype(F32) + p1_ref[...].astype(F32)).astype(BF)
    e[...] = (b_ref[:128].astype(F32) + m1_ref[...].astype(F32)).astype(BF)


def sums_of(a, b, p2, p1, m1, *after):
    return pl.pallas_call(
        sum_kernel,
        out_shape=[jax.ShapeDtypeStruct((128, 896), BF)] * 3,
        in_specs=[VMEM] * 5 + [ANY] * len(after),
        out_specs=[VMEM] * 3,
        compiler_params=PARAMS,
        cost_estimate=cost(2**18, 1),
        name="sums",
    )(a, b, p2, p1, m1, *after)


def per_device(gate, up, w, cot):
    pos = jnp.stack([lax.axis_index(a) for a in AXES]).astype(jnp.int32)
    hid = lax.all_gather(hidden_of(gate, up), RING, axis=0, tiled=True)
    near = exchange(copies_of(pos, cot, False))
    rest = copies_of(pos, cot, True, near)
    p43, m32, p2, p1, m1, here = terms_of(pos, near, w, rest)
    rest = exchange(rest)

    right, left, right2, left2 = ring_move(1), ring_move(-1), ring_move(2), ring_move(-2)
    a, b = send(p43, right2), send(m32, left2)
    o = out_of(pos, hid, w)
    c, d, e = sums_of(a, b, p2, p1, m1, o)
    c, d, e = send(c, right2), send(d, right), send(e, left)
    grad_hidden = (
        here.astype(F32) + b[128:].astype(F32) + c.astype(F32) + (d.astype(F32) + e.astype(F32))
    )
    gate_f, up_f = gate.astype(F32), up.astype(F32)
    sig = jax.nn.sigmoid(gate_f)
    grad_gate = (grad_hidden * up_f * sig * (1.0 + gate_f * (1.0 - sig))).astype(BF)
    grad_up = (grad_hidden * (gate_f * sig)).astype(BF)

    output = total_of(exchange(o.reshape(16, 64, 1024)))

    part = grad_of(pos, hid, near, rest, o, c, d, e)
    grad_weight = add(part, send(part, SWAP_CORE))
    return output, grad_gate, grad_up, grad_weight


def solution(mesh):
    mesh = Mesh(mesh.devices.reshape(DIMS), AXES)
    depth = ("zhi", "core")
    by_col, by_row = P(depth + ("col",), PLANE), P(depth + PLANE, "col")
    weight = P(PLANE, "col")
    return jax.shard_map(
        per_device,
        mesh=mesh,
        in_specs=(by_col, by_col, weight, by_row),
        out_specs=(by_row, by_col, by_col, weight),
        check_vma=False,
    )
```

```python
import functools

import jax
import jax.numpy as jnp
from jax import lax
from jax.experimental import pallas as pl
from jax.experimental.pallas import tpu as pltpu
from jax.sharding import Mesh
from jax.sharding import PartitionSpec as P

BF, F32 = jnp.bfloat16, jnp.float32
AXES = ("zhi", "core", "x", "y", "col")
DIMS = (2, 2, 4, 4, 8)
RING = ("zhi", "col")
PLANE = ("x", "y")
VMEM_LIMIT = 20 * 2**20


def flat(c):
    n = 0
    for v, d in zip(c, DIMS):
        n = n * d + v % d
    return n


def pairs(move):
    out = []
    for h in range(2):
        for k in range(2):
            for x in range(4):
                for y in range(4):
                    for c in range(8):
                        out.append((flat((h, k, x, y, c)), flat(move(h, k, x, y, c))))
    return out


def ring_move(s):
    def move(h, k, x, y, c):
        z = (h * 8 + c + s) % 16
        return (z // 8, k, x, y, z % 8)

    return pairs(move)


def half_of(h0, col, row):
    k = (row // 2 - col + 11) % 8 - 3
    return (h0 * 8 + col + k + 16) % 16 // 8


def swap_z(wanted):
    out = []
    for h in range(2):
        for k in range(2):
            for x in range(4):
                for y in range(4):
                    for c in range(8):
                        if (half_of(h, c, x * 4 + y) == h) == wanted:
                            out.append((flat((h, k, x, y, c)), flat((1 - h, k, x, y, c))))
    return out


SWAP_CORE = pairs(lambda h, k, x, y, c: (h, 1 - k, x, y, c))
SMEM = pl.BlockSpec(memory_space=pltpu.SMEM)
VMEM = pl.BlockSpec(memory_space=pltpu.VMEM)
ANY = pl.BlockSpec(memory_space=pl.ANY)
PARAMS = pltpu.CompilerParams(vmem_limit_bytes=VMEM_LIMIT)


def cost(flops, mib):
    return pl.CostEstimate(flops=flops, bytes_accessed=int(mib * 2**20), transcendentals=0)


def send(a, perm):
    return lax.ppermute(a, AXES, perm)


def hidden_kernel(gate_ref, up_ref, out_ref):
    g = gate_ref[...].astype(F32)
    out_ref[...] = (g * jax.nn.sigmoid(g) * up_ref[...].astype(F32)).astype(BF)


def hidden_of(gate, up):
    return pl.pallas_call(
        hidden_kernel,
        out_shape=jax.ShapeDtypeStruct(gate.shape, BF),
        grid=(4,),
        in_specs=[pl.BlockSpec((32, 896), lambda i: (i, 0))] * 2,
        out_specs=pl.BlockSpec((32, 896), lambda i: (i, 0)),
        compiler_params=PARAMS,
        cost_estimate=cost(2**20, 1),
        name="hidden",
    )(gate, up)


def copies_kernel(far_wanted, pos_ref, cot_ref, far_ref, *refs):
    mine = half_of(pos_ref[0], pos_ref[4], pos_ref[2] * 4 + pos_ref[3]) == pos_ref[0]

    def fill(ref):
        for i in range(16):
            refs[-1][i] = ref[...]

    pl.when(mine if far_wanted else jnp.logical_not(mine))(lambda: fill(far_ref))
    pl.when(jnp.logical_not(mine) if far_wanted else mine)(lambda: fill(cot_ref))


def copies_of(pos, cot, far_wanted, *after):
    return pl.pallas_call(
        functools.partial(copies_kernel, far_wanted),
        out_shape=jax.ShapeDtypeStruct((16, 64, 1024), BF),
        in_specs=[SMEM, VMEM, VMEM] + [ANY] * len(after),
        out_specs=VMEM,
        compiler_params=PARAMS,
        cost_estimate=cost(0, 2),
        name="copies",
    )(pos, cot, send(cot, swap_z(far_wanted)), *after)


def exchange(blocks):
    return lax.all_to_all(blocks, PLANE, 0, 0, tiled=True)


def term_kernel(pos_ref, near_ref, w_ref, *refs):
    p43, m32, p2, p1, m1, here = refs[-6:]
    col = pos_ref[4]

    def dot(k, l):
        a = jnp.concatenate([near_ref[(col + k + 8) % 8], near_ref[(col + l + 8) % 8]], axis=0)
        return lax.dot_general(
            a, w_ref[...], (((1,), (1,)), ((), ())), preferred_element_type=F32
        ).astype(BF)

    p43[...] = dot(4, 3)
    m32[...] = dot(-3, -2)
    r = dot(2, 1)
    p2[...] = r[:128]
    p1[...] = r[128:]
    r = dot(-1, 0)
    m1[...] = r[:128]
    here[...] = r[128:]


def terms_of(pos, near, w, *after):
    return pl.pallas_call(
        term_kernel,
        out_shape=[jax.ShapeDtypeStruct((n, 896), BF) for n in (256, 256, 128, 128, 128, 128)],
        in_specs=[SMEM, VMEM, VMEM] + [ANY] * len(after),
        out_specs=[VMEM] * 6,
        compiler_params=PARAMS,
        cost_estimate=cost(2 * 1024 * 896 * 1024, 8),
        name="hidden_terms",
    )(pos, near.reshape(8, 128, 1024), w, *after)


def out_kernel(pos_ref, hid_ref, w_ref, out_ref):
    at = pos_ref[0] * 1024
    for i in range(4):
        a = hid_ref[pl.ds(pl.multiple_of(at + 256 * i, 256), 256), :]
        out_ref[256 * i : 256 * i + 256] = jnp.dot(a, w_ref[...], preferred_element_type=F32).astype(BF)


def out_of(pos, hid, w):
    return pl.pallas_call(
        out_kernel,
        out_shape=jax.ShapeDtypeStruct((1024, 1024), BF),
        in_specs=[SMEM, VMEM, VMEM],
        out_specs=VMEM,
        compiler_params=PARAMS,
        cost_estimate=cost(2 * 1024 * 896 * 1024, 8),
        name="output_terms",
    )(pos, hid, w)


def total_kernel(got_ref, out_ref):
    total = got_ref[0].astype(F32)
    for i in range(1, 16):
        total = total + got_ref[i].astype(F32)
    out_ref[...] = total.astype(BF)


def total_of(got):
    return pl.pallas_call(
        total_kernel,
        grid=(4,),
        out_shape=jax.ShapeDtypeStruct((64, 1024), BF),
        in_specs=[pl.BlockSpec((16, 16, 1024), lambda i: (0, i, 0))],
        out_specs=pl.BlockSpec((16, 1024), lambda i: (i, 0)),
        compiler_params=PARAMS,
        cost_estimate=cost(2**20, 2),
        name="output_sum",
    )(got)


def grad_kernel(pos_ref, hid_ref, near_ref, rest_ref, *refs):
    out_ref, cot_ref = refs[-2:]
    h0, col = pos_ref[0], pos_ref[4]

    @pl.when(pl.program_id(0) == 0)
    def _():
        for r in range(16):
            h = half_of(h0, col, r)
            cot_ref[pl.ds(pl.multiple_of(h * 1024 + r * 64, 64), 64), :] = near_ref[r]
            cot_ref[pl.ds(pl.multiple_of((1 - h) * 1024 + r * 64, 64), 64), :] = rest_ref[r]

    n = pl.multiple_of(pl.program_id(0) * 256, 256)
    out_ref[...] = lax.dot_general(
        hid_ref[...], cot_ref[:, pl.ds(n, 256)], (((0,), (0,)), ((), ())), preferred_element_type=F32
    ).astype(BF)


def grad_of(pos, hid, near, rest, *after):
    return pl.pallas_call(
        grad_kernel,
        grid=(4,),
        out_shape=jax.ShapeDtypeStruct((896, 1024), BF),
        in_specs=[SMEM, VMEM, VMEM, VMEM] + [ANY] * len(after),
        out_specs=pl.BlockSpec((896, 256), lambda n: (0, n)),
        scratch_shapes=[pltpu.VMEM((2048, 1024), BF)],
        compiler_params=PARAMS,
        cost_estimate=cost(2 * 2048 * 896 * 1024, 10),
        name="weight_terms",
    )(pos, hid, near, rest, *after)


def pair_kernel(a_ref, b_ref, *refs):
    refs[-1][...] = (a_ref[...].astype(F32) + b_ref[...].astype(F32)).astype(BF)


def pair_of(a, b, *after):
    block = pl.BlockSpec((224, 1024), lambda i: (i, 0))
    return pl.pallas_call(
        pair_kernel,
        grid=(4,),
        out_shape=jax.ShapeDtypeStruct((896, 1024), BF),
        in_specs=[block] * 2 + [ANY] * len(after),
        out_specs=block,
        compiler_params=PARAMS,
        cost_estimate=cost(2**20, 5),
        name="weight_sum",
    )(a, b, *after)


def ends_kernel(gate_ref, up_ref, here_ref, b_ref, c_ref, d_ref, e_ref, *refs):
    grad = here_ref[...].astype(F32) + b_ref[128:].astype(F32) + c_ref[...].astype(F32)
    grad = grad + (d_ref[...].astype(F32) + e_ref[...].astype(F32))
    g, u = gate_ref[...].astype(F32), up_ref[...].astype(F32)
    sig = jax.nn.sigmoid(g)
    refs[-2][...] = (grad * u * sig * (1.0 + g * (1.0 - sig))).astype(BF)
    refs[-1][...] = (grad * (g * sig)).astype(BF)


def ends_of(gate, up, here, b, c, d, e, *after):
    return pl.pallas_call(
        ends_kernel,
        out_shape=[jax.ShapeDtypeStruct((128, 896), BF)] * 2,
        in_specs=[VMEM] * 7 + [ANY] * len(after),
        out_specs=[VMEM] * 2,
        compiler_params=PARAMS,
        cost_estimate=cost(2**21, 2),
        name="gradients",
    )(gate, up, here, b, c, d, e, *after)


def sum_kernel(a_ref, b_ref, p2_ref, p1_ref, m1_ref, *refs):
    c, d, e = refs[-3:]
    c[...] = (a_ref[:128].astype(F32) + p2_ref[...].astype(F32)).astype(BF)
    d[...] = (a_ref[128:].astype(F32) + p1_ref[...].astype(F32)).astype(BF)
    e[...] = (b_ref[:128].astype(F32) + m1_ref[...].astype(F32)).astype(BF)


def sums_of(a, b, p2, p1, m1, *after):
    return pl.pallas_call(
        sum_kernel,
        out_shape=[jax.ShapeDtypeStruct((128, 896), BF)] * 3,
        in_specs=[VMEM] * 5 + [ANY] * len(after),
        out_specs=[VMEM] * 3,
        compiler_params=PARAMS,
        cost_estimate=cost(2**18, 1),
        name="sums",
    )(a, b, p2, p1, m1, *after)


def per_device(gate, up, w, cot):
    pos = jnp.stack([lax.axis_index(a) for a in AXES]).astype(jnp.int32)
    hid = lax.all_gather(hidden_of(gate, up), RING, axis=0, tiled=True)
    near = exchange(copies_of(pos, cot, False))
    rest = copies_of(pos, cot, True, near)
    p43, m32, p2, p1, m1, here = terms_of(pos, near, w, rest)
    rest = exchange(rest)

    right, left, right2, left2 = ring_move(1), ring_move(-1), ring_move(2), ring_move(-2)
    a, b = send(p43, right2), send(m32, left2)
    o = out_of(pos, hid, w)
    c, d, e = sums_of(a, b, p2, p1, m1)
    c, d, e = send(c, right2), send(d, right), send(e, left)
    output = total_of(exchange(o.reshape(16, 64, 1024)))
    grad_gate, grad_up = ends_of(gate, up, here, b, c, d, e, output)

    part = grad_of(pos, hid, near, rest, o, a, b)
    grad_weight = pair_of(part, send(part, SWAP_CORE), output)
    return output, grad_gate, grad_up, grad_weight


def solution(mesh):
    mesh = Mesh(mesh.devices.reshape(DIMS), AXES)
    depth = ("zhi", "core")
    by_col, by_row = P(depth + ("col",), PLANE), P(depth + PLANE, "col")
    weight = P(PLANE, "col")
    return jax.shard_map(
        per_device,
        mesh=mesh,
        in_specs=(by_col, by_col, weight, by_row),
        out_specs=(by_row, by_col, by_col, weight),
        check_vma=False,
    )
```

```python
import functools

import jax
import jax.numpy as jnp
from jax import lax
from jax.experimental import pallas as pl
from jax.experimental.pallas import tpu as pltpu
from jax.sharding import Mesh
from jax.sharding import PartitionSpec as P

BF, F32 = jnp.bfloat16, jnp.float32
AXES = ("zhi", "core", "x", "y", "col")
DIMS = (2, 2, 4, 4, 8)
RING = ("zhi", "col")
PLANE = ("x", "y")
VMEM_LIMIT = 20 * 2**20


def flat(c):
    n = 0
    for v, d in zip(c, DIMS):
        n = n * d + v % d
    return n


def pairs(move):
    out = []
    for h in range(2):
        for k in range(2):
            for x in range(4):
                for y in range(4):
                    for c in range(8):
                        out.append((flat((h, k, x, y, c)), flat(move(h, k, x, y, c))))
    return out


def ring_move(s):
    def move(h, k, x, y, c):
        z = (h * 8 + c + s) % 16
        return (z // 8, k, x, y, z % 8)

    return pairs(move)


def half_of(h0, col, row):
    k = (row // 2 - col + 11) % 8 - 3
    return (h0 * 8 + col + k + 16) % 16 // 8


def swap_z(wanted):
    out = []
    for h in range(2):
        for k in range(2):
            for x in range(4):
                for y in range(4):
                    for c in range(8):
                        if (half_of(h, c, x * 4 + y) == h) == wanted:
                            out.append((flat((h, k, x, y, c)), flat((1 - h, k, x, y, c))))
    return out


SWAP_CORE = pairs(lambda h, k, x, y, c: (h, 1 - k, x, y, c))
SMEM = pl.BlockSpec(memory_space=pltpu.SMEM)
VMEM = pl.BlockSpec(memory_space=pltpu.VMEM)
ANY = pl.BlockSpec(memory_space=pl.ANY)
PARAMS = pltpu.CompilerParams(vmem_limit_bytes=VMEM_LIMIT)


def cost(flops, mib):
    return pl.CostEstimate(flops=flops, bytes_accessed=int(mib * 2**20), transcendentals=0)


def send(a, perm):
    return lax.ppermute(a, AXES, perm)


def hidden_kernel(gate_ref, up_ref, out_ref):
    g = gate_ref[...].astype(F32)
    out_ref[...] = (g * jax.nn.sigmoid(g) * up_ref[...].astype(F32)).astype(BF)


def hidden_of(gate, up):
    return pl.pallas_call(
        hidden_kernel,
        out_shape=jax.ShapeDtypeStruct(gate.shape, BF),
        grid=(4,),
        in_specs=[pl.BlockSpec((32, 896), lambda i: (i, 0))] * 2,
        out_specs=pl.BlockSpec((32, 896), lambda i: (i, 0)),
        compiler_params=PARAMS,
        cost_estimate=cost(2**20, 1),
        name="hidden",
    )(gate, up)


def copies_kernel(far_wanted, pos_ref, cot_ref, far_ref, *refs):
    mine = half_of(pos_ref[0], pos_ref[4], pos_ref[2] * 4 + pos_ref[3]) == pos_ref[0]

    def fill(ref):
        for i in range(16):
            refs[-1][i] = ref[...]

    pl.when(mine if far_wanted else jnp.logical_not(mine))(lambda: fill(far_ref))
    pl.when(jnp.logical_not(mine) if far_wanted else mine)(lambda: fill(cot_ref))


def copies_of(pos, cot, far_wanted, *after):
    return pl.pallas_call(
        functools.partial(copies_kernel, far_wanted),
        out_shape=jax.ShapeDtypeStruct((16, 64, 1024), BF),
        in_specs=[SMEM, VMEM, VMEM] + [ANY] * len(after),
        out_specs=VMEM,
        compiler_params=PARAMS,
        cost_estimate=cost(0, 2),
        name="copies",
    )(pos, cot, send(cot, swap_z(far_wanted)), *after)


def exchange(blocks):
    return lax.all_to_all(blocks, PLANE, 0, 0, tiled=True)


def term_kernel(parts, pos_ref, near_ref, w_ref, *refs):
    outs = refs[len(refs) - len(parts) :]
    for part, out in zip(parts, outs):
        rows = [near_ref[(pos_ref[4] + k + 8) % 8] for k in part]
        out[...] = lax.dot_general(
            rows[0] if len(rows) == 1 else jnp.concatenate(rows, axis=0),
            w_ref[...],
            (((1,), (1,)), ((), ())),
            preferred_element_type=F32,
        ).astype(BF)


def terms_of(parts, pos, near, w, *after):
    n = sum(len(p) for p in parts)
    return pl.pallas_call(
        functools.partial(term_kernel, parts),
        out_shape=[jax.ShapeDtypeStruct((128 * len(p), 896), BF) for p in parts],
        in_specs=[SMEM, VMEM, VMEM] + [ANY] * len(after),
        out_specs=[VMEM] * len(parts),
        compiler_params=PARAMS,
        cost_estimate=cost(2 * 128 * n * 896 * 1024, 4),
        name="hidden_terms",
    )(pos, near.reshape(8, 128, 1024), w, *after)


def out_kernel(pos_ref, hid_ref, w_ref, out_ref):
    at = pos_ref[0] * 1024
    for i in range(4):
        a = hid_ref[pl.ds(pl.multiple_of(at + 256 * i, 256), 256), :]
        out_ref[256 * i : 256 * i + 256] = jnp.dot(a, w_ref[...], preferred_element_type=F32).astype(BF)


def out_of(pos, hid, w):
    return pl.pallas_call(
        out_kernel,
        out_shape=jax.ShapeDtypeStruct((1024, 1024), BF),
        in_specs=[SMEM, VMEM, VMEM],
        out_specs=VMEM,
        compiler_params=PARAMS,
        cost_estimate=cost(2 * 1024 * 896 * 1024, 8),
        name="output_terms",
    )(pos, hid, w)


def total_kernel(got_ref, out_ref):
    total = got_ref[0].astype(F32)
    for i in range(1, 16):
        total = total + got_ref[i].astype(F32)
    out_ref[...] = total.astype(BF)


def total_of(got):
    return pl.pallas_call(
        total_kernel,
        grid=(4,),
        out_shape=jax.ShapeDtypeStruct((64, 1024), BF),
        in_specs=[pl.BlockSpec((16, 16, 1024), lambda i: (0, i, 0))],
        out_specs=pl.BlockSpec((16, 1024), lambda i: (i, 0)),
        compiler_params=PARAMS,
        cost_estimate=cost(2**20, 2),
        name="output_sum",
    )(got)


def grad_kernel(pos_ref, hid_ref, near_ref, rest_ref, *refs):
    out_ref, cot_ref = refs[-2:]
    h0, col = pos_ref[0], pos_ref[4]

    @pl.when(pl.program_id(0) == 0)
    def _():
        for r in range(16):
            h = half_of(h0, col, r)
            cot_ref[pl.ds(pl.multiple_of(h * 1024 + r * 64, 64), 64), :] = near_ref[r]
            cot_ref[pl.ds(pl.multiple_of((1 - h) * 1024 + r * 64, 64), 64), :] = rest_ref[r]

    n = pl.multiple_of(pl.program_id(0) * 256, 256)
    out_ref[...] = lax.dot_general(
        hid_ref[...], cot_ref[:, pl.ds(n, 256)], (((0,), (0,)), ((), ())), preferred_element_type=F32
    ).astype(BF)


def grad_of(pos, hid, near, rest, *after):
    return pl.pallas_call(
        grad_kernel,
        grid=(4,),
        out_shape=jax.ShapeDtypeStruct((896, 1024), BF),
        in_specs=[SMEM, VMEM, VMEM, VMEM] + [ANY] * len(after),
        out_specs=pl.BlockSpec((896, 256), lambda n: (0, n)),
        scratch_shapes=[pltpu.VMEM((2048, 1024), BF)],
        compiler_params=PARAMS,
        cost_estimate=cost(2 * 2048 * 896 * 1024, 10),
        name="weight_terms",
    )(pos, hid, near, rest, *after)


def pair_kernel(a_ref, b_ref, *refs):
    refs[-1][...] = (a_ref[...].astype(F32) + b_ref[...].astype(F32)).astype(BF)


def pair_of(a, b, *after):
    block = pl.BlockSpec((224, 1024), lambda i: (i, 0))
    return pl.pallas_call(
        pair_kernel,
        grid=(4,),
        out_shape=jax.ShapeDtypeStruct((896, 1024), BF),
        in_specs=[block] * 2 + [ANY] * len(after),
        out_specs=block,
        compiler_params=PARAMS,
        cost_estimate=cost(2**20, 5),
        name="weight_sum",
    )(a, b, *after)


def ends_kernel(gate_ref, up_ref, here_ref, b_ref, c_ref, d_ref, e_ref, *refs):
    grad = here_ref[...].astype(F32) + b_ref[128:].astype(F32) + c_ref[...].astype(F32)
    grad = grad + (d_ref[...].astype(F32) + e_ref[...].astype(F32))
    g, u = gate_ref[...].astype(F32), up_ref[...].astype(F32)
    sig = jax.nn.sigmoid(g)
    refs[-2][...] = (grad * u * sig * (1.0 + g * (1.0 - sig))).astype(BF)
    refs[-1][...] = (grad * (g * sig)).astype(BF)


def ends_of(gate, up, here, b, c, d, e, *after):
    return pl.pallas_call(
        ends_kernel,
        out_shape=[jax.ShapeDtypeStruct((128, 896), BF)] * 2,
        in_specs=[VMEM] * 7 + [ANY] * len(after),
        out_specs=[VMEM] * 2,
        compiler_params=PARAMS,
        cost_estimate=cost(2**21, 2),
        name="gradients",
    )(gate, up, here, b, c, d, e, *after)


def sum_kernel(a_ref, p_ref, q_ref, c_ref, d_ref):
    c_ref[...] = (a_ref[:128].astype(F32) + p_ref[...].astype(F32)).astype(BF)
    d_ref[...] = (a_ref[128:].astype(F32) + q_ref[...].astype(F32)).astype(BF)


def sums_of(a, p, q):
    return pl.pallas_call(
        sum_kernel,
        out_shape=[jax.ShapeDtypeStruct((128, 896), BF)] * 2,
        in_specs=[VMEM] * 3,
        out_specs=[VMEM] * 2,
        compiler_params=PARAMS,
        cost_estimate=cost(2**18, 1),
        name="sums",
    )(a, p, q)


def per_device(gate, up, w, cot):
    pos = jnp.stack([lax.axis_index(a) for a in AXES]).astype(jnp.int32)
    hid = lax.all_gather(hidden_of(gate, up), RING, axis=0, tiled=True)
    near = exchange(copies_of(pos, cot, False))
    rest = copies_of(pos, cot, True, near)
    p43, p2, p1, here = terms_of(((4, 3), (2,), (1,), (0,)), pos, near, w, rest)
    rest = exchange(rest)

    right, left, right2, left2 = ring_move(1), ring_move(-1), ring_move(2), ring_move(-2)
    a = send(p43, right2)
    o = out_of(pos, hid, w)
    m32, m1 = terms_of(((-3, -2), (-1,)), pos, near, w, o)
    b = send(m32, left2)
    c, d = sums_of(a, p2, p1)
    e = (b[:128].astype(F32) + m1.astype(F32)).astype(BF)
    c, d, e = send(c, right2), send(d, right), send(e, left)
    output = total_of(exchange(o.reshape(16, 64, 1024)))
    grad_gate, grad_up = ends_of(gate, up, here, b, c, d, e, output)

    part = grad_of(pos, hid, near, rest, o, c, d)
    grad_weight = pair_of(part, send(part, SWAP_CORE), output)
    return output, grad_gate, grad_up, grad_weight


def solution(mesh):
    mesh = Mesh(mesh.devices.reshape(DIMS), AXES)
    depth = ("zhi", "core")
    by_col, by_row = P(depth + ("col",), PLANE), P(depth + PLANE, "col")
    weight = P(PLANE, "col")
    return jax.shard_map(
        per_device,
        mesh=mesh,
        in_specs=(by_col, by_col, weight, by_row),
        out_specs=(by_row, by_col, by_col, weight),
        check_vma=False,
    )
```

```python
import functools

import jax
import jax.numpy as jnp
from jax import lax
from jax.experimental import pallas as pl
from jax.experimental.pallas import tpu as pltpu
from jax.sharding import Mesh
from jax.sharding import PartitionSpec as P

BF, F32 = jnp.bfloat16, jnp.float32
AXES = ("zhi", "core", "x", "y", "col")
DIMS = (2, 2, 4, 4, 8)
RING = ("zhi", "col")
PLANE = ("x", "y")
VMEM_LIMIT = 20 * 2**20


def flat(c):
    n = 0
    for v, d in zip(c, DIMS):
        n = n * d + v % d
    return n


def pairs(move):
    out = []
    for h in range(2):
        for k in range(2):
            for x in range(4):
                for y in range(4):
                    for c in range(8):
                        out.append((flat((h, k, x, y, c)), flat(move(h, k, x, y, c))))
    return out


def ring_move(s):
    def move(h, k, x, y, c):
        z = (h * 8 + c + s) % 16
        return (z // 8, k, x, y, z % 8)

    return pairs(move)


def half_of(h0, col, row):
    k = (row // 2 - col + 11) % 8 - 3
    return (h0 * 8 + col + k + 16) % 16 // 8


def swap_z(wanted):
    out = []
    for h in range(2):
        for k in range(2):
            for x in range(4):
                for y in range(4):
                    for c in range(8):
                        if (half_of(h, c, x * 4 + y) == h) == wanted:
                            out.append((flat((h, k, x, y, c)), flat((1 - h, k, x, y, c))))
    return out


SWAP_CORE = pairs(lambda h, k, x, y, c: (h, 1 - k, x, y, c))
SMEM = pl.BlockSpec(memory_space=pltpu.SMEM)
VMEM = pl.BlockSpec(memory_space=pltpu.VMEM)
ANY = pl.BlockSpec(memory_space=pl.ANY)
PARAMS = pltpu.CompilerParams(vmem_limit_bytes=VMEM_LIMIT)


def cost(flops, mib):
    return pl.CostEstimate(flops=flops, bytes_accessed=int(mib * 2**20), transcendentals=0)


def send(a, perm):
    return lax.ppermute(a, AXES, perm)


def hidden_kernel(gate_ref, up_ref, out_ref):
    g = gate_ref[...].astype(F32)
    out_ref[...] = (g * jax.nn.sigmoid(g) * up_ref[...].astype(F32)).astype(BF)


def hidden_of(gate, up):
    return pl.pallas_call(
        hidden_kernel,
        out_shape=jax.ShapeDtypeStruct(gate.shape, BF),
        grid=(4,),
        in_specs=[pl.BlockSpec((32, 896), lambda i: (i, 0))] * 2,
        out_specs=pl.BlockSpec((32, 896), lambda i: (i, 0)),
        compiler_params=PARAMS,
        cost_estimate=cost(2**20, 1),
        name="hidden",
    )(gate, up)


def copies_kernel(far_wanted, pos_ref, cot_ref, far_ref, *refs):
    mine = half_of(pos_ref[0], pos_ref[4], pos_ref[2] * 4 + pos_ref[3]) == pos_ref[0]

    def fill(ref):
        for i in range(16):
            refs[-1][i] = ref[...]

    pl.when(mine if far_wanted else jnp.logical_not(mine))(lambda: fill(far_ref))
    pl.when(jnp.logical_not(mine) if far_wanted else mine)(lambda: fill(cot_ref))


def copies_of(pos, cot, far, far_wanted, *after):
    return pl.pallas_call(
        functools.partial(copies_kernel, far_wanted),
        out_shape=jax.ShapeDtypeStruct((16, 64, 1024), BF),
        in_specs=[SMEM, VMEM, VMEM] + [ANY] * len(after),
        out_specs=VMEM,
        compiler_params=PARAMS,
        cost_estimate=cost(0, 2),
        name="copies",
    )(pos, cot, far, *after)


def exchange(blocks):
    return lax.all_to_all(blocks, PLANE, 0, 0, tiled=True)


def term_kernel(parts, pos_ref, near_ref, w_ref, *refs):
    outs = refs[len(refs) - len(parts) :]
    for part, out in zip(parts, outs):
        rows = [near_ref[(pos_ref[4] + k + 8) % 8] for k in part]
        out[...] = lax.dot_general(
            rows[0] if len(rows) == 1 else jnp.concatenate(rows, axis=0),
            w_ref[...],
            (((1,), (1,)), ((), ())),
            preferred_element_type=F32,
        ).astype(BF)


def terms_of(parts, pos, near, w, *after):
    n = sum(len(p) for p in parts)
    return pl.pallas_call(
        functools.partial(term_kernel, parts),
        out_shape=[jax.ShapeDtypeStruct((128 * len(p), 896), BF) for p in parts],
        in_specs=[SMEM, VMEM, VMEM] + [ANY] * len(after),
        out_specs=[VMEM] * len(parts),
        compiler_params=PARAMS,
        cost_estimate=cost(2 * 128 * n * 896 * 1024, 4),
        name="hidden_terms",
    )(pos, near.reshape(8, 128, 1024), w, *after)


def out_kernel(pos_ref, hid_ref, w_ref, out_ref):
    at = pos_ref[0] * 1024
    for i in range(4):
        a = hid_ref[pl.ds(pl.multiple_of(at + 256 * i, 256), 256), :]
        out_ref[256 * i : 256 * i + 256] = jnp.dot(a, w_ref[...], preferred_element_type=F32).astype(BF)


def out_of(pos, hid, w):
    return pl.pallas_call(
        out_kernel,
        out_shape=jax.ShapeDtypeStruct((1024, 1024), BF),
        in_specs=[SMEM, VMEM, VMEM],
        out_specs=VMEM,
        compiler_params=PARAMS,
        cost_estimate=cost(2 * 1024 * 896 * 1024, 8),
        name="output_terms",
    )(pos, hid, w)


def total_kernel(got_ref, out_ref):
    total = got_ref[0].astype(F32)
    for i in range(1, 16):
        total = total + got_ref[i].astype(F32)
    out_ref[...] = total.astype(BF)


def total_of(got):
    return pl.pallas_call(
        total_kernel,
        grid=(4,),
        out_shape=jax.ShapeDtypeStruct((64, 1024), BF),
        in_specs=[pl.BlockSpec((16, 16, 1024), lambda i: (0, i, 0))],
        out_specs=pl.BlockSpec((16, 1024), lambda i: (i, 0)),
        compiler_params=PARAMS,
        cost_estimate=cost(2**20, 2),
        name="output_sum",
    )(got)


def grad_kernel(pos_ref, hid_ref, near_ref, rest_ref, *refs):
    out_ref, cot_ref = refs[-2:]
    h0, col = pos_ref[0], pos_ref[4]

    @pl.when(pl.program_id(0) == 0)
    def _():
        for r in range(16):
            h = half_of(h0, col, r)
            cot_ref[pl.ds(pl.multiple_of(h * 1024 + r * 64, 64), 64), :] = near_ref[r]
            cot_ref[pl.ds(pl.multiple_of((1 - h) * 1024 + r * 64, 64), 64), :] = rest_ref[r]

    n = pl.multiple_of(pl.program_id(0) * 256, 256)
    out_ref[...] = lax.dot_general(
        hid_ref[...], cot_ref[:, pl.ds(n, 256)], (((0,), (0,)), ((), ())), preferred_element_type=F32
    ).astype(BF)


def grad_of(pos, hid, near, rest, *after):
    return pl.pallas_call(
        grad_kernel,
        grid=(4,),
        out_shape=jax.ShapeDtypeStruct((896, 1024), BF),
        in_specs=[SMEM, VMEM, VMEM, VMEM] + [ANY] * len(after),
        out_specs=pl.BlockSpec((896, 256), lambda n: (0, n)),
        scratch_shapes=[pltpu.VMEM((2048, 1024), BF)],
        compiler_params=PARAMS,
        cost_estimate=cost(2 * 2048 * 896 * 1024, 10),
        name="weight_terms",
    )(pos, hid, near, rest, *after)


def pair_kernel(a_ref, b_ref, *refs):
    refs[-1][...] = (a_ref[...].astype(F32) + b_ref[...].astype(F32)).astype(BF)


def pair_of(a, b, *after):
    block = pl.BlockSpec((224, 1024), lambda i: (i, 0))
    return pl.pallas_call(
        pair_kernel,
        grid=(4,),
        out_shape=jax.ShapeDtypeStruct((896, 1024), BF),
        in_specs=[block] * 2 + [ANY] * len(after),
        out_specs=block,
        compiler_params=PARAMS,
        cost_estimate=cost(2**20, 5),
        name="weight_sum",
    )(a, b, *after)


def ends_kernel(gate_ref, up_ref, here_ref, a_ref, b_ref, *refs):
    grad = here_ref[...].astype(F32) + a_ref[...].astype(F32) + b_ref[...].astype(F32)
    g, u = gate_ref[...].astype(F32), up_ref[...].astype(F32)
    sig = jax.nn.sigmoid(g)
    refs[-2][...] = (grad * u * sig * (1.0 + g * (1.0 - sig))).astype(BF)
    refs[-1][...] = (grad * (g * sig)).astype(BF)


def ends_of(gate, up, here, a, b, *after):
    return pl.pallas_call(
        ends_kernel,
        out_shape=[jax.ShapeDtypeStruct((128, 896), BF)] * 2,
        in_specs=[VMEM] * 5 + [ANY] * len(after),
        out_specs=[VMEM] * 2,
        compiler_params=PARAMS,
        cost_estimate=cost(2**21, 2),
        name="gradients",
    )(gate, up, here, a, b, *after)


def add_kernel(*refs):
    n = len(refs) // 3
    for i in range(n):
        refs[2 * n + i][...] = (refs[2 * i][...].astype(F32) + refs[2 * i + 1][...].astype(F32)).astype(BF)


def add(*pairs_of):
    out = pl.pallas_call(
        add_kernel,
        out_shape=[jax.ShapeDtypeStruct((128, 896), BF)] * len(pairs_of),
        in_specs=[VMEM] * (2 * len(pairs_of)),
        out_specs=[VMEM] * len(pairs_of),
        compiler_params=PARAMS,
        cost_estimate=cost(2**18, 1),
        name="sums",
    )(*[v for p in pairs_of for v in p])
    return out


def per_device(gate, up, w, cot):
    pos = jnp.stack([lax.axis_index(a) for a in AXES]).astype(jnp.int32)
    hid = lax.all_gather(hidden_of(gate, up), RING, axis=0, tiled=True)
    near = exchange(copies_of(pos, cot, send(cot, swap_z(False)), False))
    far = send(cot, swap_z(True))
    parts = ((4,), (3,), (-3,), (2,), (-2,), (1,), (-1,), (0,))
    p4, p3, m3, p2, m2, p1, m1, here = terms_of(parts, pos, near, w, far)

    right, left = ring_move(1), ring_move(-1)
    a = send(p4, right)
    a, = add((a, p3))
    a, b = send(a, right), send(m3, left)
    rest = exchange(copies_of(pos, cot, far, True, a))
    a, b = add((a, p2), (b, m2))
    a, b = send(a, right), send(b, left)
    a, b = add((a, p1), (b, m1))
    a, b = send(a, right), send(b, left)

    o = out_of(pos, hid, w)
    output = total_of(exchange(o.reshape(16, 64, 1024)))
    grad_gate, grad_up = ends_of(gate, up, here, a, b, output)

    part = grad_of(pos, hid, near, rest, o, a, b)
    grad_weight = pair_of(part, send(part, SWAP_CORE))
    return output, grad_gate, grad_up, grad_weight


def solution(mesh):
    mesh = Mesh(mesh.devices.reshape(DIMS), AXES)
    depth = ("zhi", "core")
    by_col, by_row = P(depth + ("col",), PLANE), P(depth + PLANE, "col")
    weight = P(PLANE, "col")
    return jax.shard_map(
        per_device,
        mesh=mesh,
        in_specs=(by_col, by_col, weight, by_row),
        out_specs=(by_row, by_col, by_col, weight),
        check_vma=False,
    )
```

```python
import functools

import jax
import jax.numpy as jnp
from jax import lax
from jax.experimental import pallas as pl
from jax.experimental.pallas import tpu as pltpu
from jax.sharding import Mesh
from jax.sharding import PartitionSpec as P

BF, F32 = jnp.bfloat16, jnp.float32
AXES = ("zhi", "core", "x", "y", "col")
DIMS = (2, 2, 4, 4, 8)
RING = ("zhi", "col")
PLANE = ("x", "y")
VMEM_LIMIT = 20 * 2**20


def flat(c):
    n = 0
    for v, d in zip(c, DIMS):
        n = n * d + v % d
    return n


def pairs(move):
    out = []
    for h in range(2):
        for k in range(2):
            for x in range(4):
                for y in range(4):
                    for c in range(8):
                        out.append((flat((h, k, x, y, c)), flat(move(h, k, x, y, c))))
    return out


def ring_move(s):
    def move(h, k, x, y, c):
        z = (h * 8 + c + s) % 16
        return (z // 8, k, x, y, z % 8)

    return pairs(move)


def half_of(h0, col, row):
    k = (row // 2 - col + 11) % 8 - 3
    return (h0 * 8 + col + k + 16) % 16 // 8


def swap_z(wanted):
    out = []
    for h in range(2):
        for k in range(2):
            for x in range(4):
                for y in range(4):
                    for c in range(8):
                        if (half_of(h, c, x * 4 + y) == h) == wanted:
                            out.append((flat((h, k, x, y, c)), flat((1 - h, k, x, y, c))))
    return out


SWAP_CORE = pairs(lambda h, k, x, y, c: (h, 1 - k, x, y, c))
SMEM = pl.BlockSpec(memory_space=pltpu.SMEM)
VMEM = pl.BlockSpec(memory_space=pltpu.VMEM)
ANY = pl.BlockSpec(memory_space=pl.ANY)
PARAMS = pltpu.CompilerParams(vmem_limit_bytes=VMEM_LIMIT)
ALONE = pltpu.CompilerParams(vmem_limit_bytes=60 * 2**20)


def cost(flops, mib):
    return pl.CostEstimate(flops=flops, bytes_accessed=int(mib * 2**20), transcendentals=0)


def send(a, perm):
    return lax.ppermute(a, AXES, perm)


def started(moves):
    for m in moves:
        m.start()
    return moves


def hidden_kernel(gate_ref, up_ref, out_ref, g_ref, u_ref, sems):
    moves = started(
        [
            pltpu.make_async_copy(src.at[pl.ds(64 * i, 64)], dst.at[pl.ds(64 * i, 64)], sems.at[2 * i + n])
            for i in range(2)
            for n, (src, dst) in enumerate(((gate_ref, g_ref), (up_ref, u_ref)))
        ]
    )
    for i in range(2):
        moves[2 * i].wait()
        moves[2 * i + 1].wait()
        s = slice(64 * i, 64 * i + 64)
        g = g_ref[s].astype(F32)
        out_ref[s] = (g * jax.nn.sigmoid(g) * u_ref[s].astype(F32)).astype(BF)


def hidden_of(gate, up):
    return pl.pallas_call(
        hidden_kernel,
        out_shape=jax.ShapeDtypeStruct(gate.shape, BF),
        in_specs=[ANY, ANY],
        out_specs=VMEM,
        scratch_shapes=[pltpu.VMEM((128, 896), BF), pltpu.VMEM((128, 896), BF), pltpu.SemaphoreType.DMA((4,))],
        compiler_params=ALONE,
        cost_estimate=cost(2**20, 1),
        name="hidden",
    )(gate, up)


def copies_kernel(far_wanted, pos_ref, cot_ref, far_ref, *refs):
    mine = half_of(pos_ref[0], pos_ref[4], pos_ref[2] * 4 + pos_ref[3]) == pos_ref[0]

    def fill(ref):
        for i in range(16):
            refs[-1][i] = ref[...]

    pl.when(mine if far_wanted else jnp.logical_not(mine))(lambda: fill(far_ref))
    pl.when(jnp.logical_not(mine) if far_wanted else mine)(lambda: fill(cot_ref))


def copies_of(pos, cot, far_wanted, *after):
    return pl.pallas_call(
        functools.partial(copies_kernel, far_wanted),
        out_shape=jax.ShapeDtypeStruct((16, 64, 1024), BF),
        in_specs=[SMEM, VMEM, VMEM] + [ANY] * len(after),
        out_specs=VMEM,
        compiler_params=PARAMS,
        cost_estimate=cost(0, 2),
        name="copies",
    )(pos, cot, send(cot, swap_z(far_wanted)), *after)


def exchange(blocks):
    return lax.all_to_all(blocks, PLANE, 0, 0, tiled=True)


def term_kernel(pos_ref, near_ref, w_ref, *refs):
    p43, m32, p2, p1, m1, here = refs[-6:]
    col = pos_ref[4]

    def dot(k, l):
        a = jnp.concatenate([near_ref[(col + k + 8) % 8], near_ref[(col + l + 8) % 8]], axis=0)
        return lax.dot_general(
            a, w_ref[...], (((1,), (1,)), ((), ())), preferred_element_type=F32
        ).astype(BF)

    p43[...] = dot(4, 3)
    m32[...] = dot(-3, -2)
    r = dot(2, 1)
    p2[...] = r[:128]
    p1[...] = r[128:]
    r = dot(-1, 0)
    m1[...] = r[:128]
    here[...] = r[128:]


def terms_of(pos, near, w, *after):
    return pl.pallas_call(
        term_kernel,
        out_shape=[jax.ShapeDtypeStruct((n, 896), BF) for n in (256, 256, 128, 128, 128, 128)],
        in_specs=[SMEM, VMEM, VMEM] + [ANY] * len(after),
        out_specs=[VMEM] * 6,
        compiler_params=PARAMS,
        cost_estimate=cost(2 * 1024 * 896 * 1024, 8),
        name="hidden_terms",
    )(pos, near.reshape(8, 128, 1024), w, *after)


def out_kernel(pos_ref, hid_ref, w_ref, out_ref):
    at = pos_ref[0] * 1024
    for i in range(4):
        a = hid_ref[pl.ds(pl.multiple_of(at + 256 * i, 256), 256), :]
        out_ref[256 * i : 256 * i + 256] = jnp.dot(a, w_ref[...], preferred_element_type=F32).astype(BF)


def out_of(pos, hid, w):
    return pl.pallas_call(
        out_kernel,
        out_shape=jax.ShapeDtypeStruct((1024, 1024), BF),
        in_specs=[SMEM, VMEM, VMEM],
        out_specs=VMEM,
        compiler_params=PARAMS,
        cost_estimate=cost(2 * 1024 * 896 * 1024, 8),
        name="output_terms",
    )(pos, hid, w)


def total_kernel(got_ref, out_ref):
    total = got_ref[0].astype(F32)
    for i in range(1, 16):
        total = total + got_ref[i].astype(F32)
    out_ref[...] = total.astype(BF)


def total_of(got):
    return pl.pallas_call(
        total_kernel,
        grid=(4,),
        out_shape=jax.ShapeDtypeStruct((64, 1024), BF),
        in_specs=[pl.BlockSpec((16, 16, 1024), lambda i: (0, i, 0))],
        out_specs=pl.BlockSpec((16, 1024), lambda i: (i, 0)),
        compiler_params=PARAMS,
        cost_estimate=cost(2**20, 2),
        name="output_sum",
    )(got)


def grad_kernel(pos_ref, hid_ref, near_ref, rest_ref, *refs):
    out_ref, cot_ref = refs[-2:]
    h0, col = pos_ref[0], pos_ref[4]

    @pl.when(pl.program_id(0) == 0)
    def _():
        for r in range(16):
            h = half_of(h0, col, r)
            cot_ref[pl.ds(pl.multiple_of(h * 1024 + r * 64, 64), 64), :] = near_ref[r]
            cot_ref[pl.ds(pl.multiple_of((1 - h) * 1024 + r * 64, 64), 64), :] = rest_ref[r]

    n = pl.multiple_of(pl.program_id(0) * 256, 256)
    out_ref[...] = lax.dot_general(
        hid_ref[...], cot_ref[:, pl.ds(n, 256)], (((0,), (0,)), ((), ())), preferred_element_type=F32
    ).astype(BF)


def grad_of(pos, hid, near, rest, *after):
    return pl.pallas_call(
        grad_kernel,
        grid=(4,),
        out_shape=jax.ShapeDtypeStruct((896, 1024), BF),
        in_specs=[SMEM, VMEM, VMEM, VMEM] + [ANY] * len(after),
        out_specs=pl.BlockSpec((896, 256), lambda n: (0, n)),
        scratch_shapes=[pltpu.VMEM((2048, 1024), BF)],
        compiler_params=PARAMS,
        cost_estimate=cost(2 * 2048 * 896 * 1024, 10),
        name="weight_terms",
    )(pos, hid, near, rest, *after)


def pair_kernel(a_ref, b_ref, *refs):
    refs[-1][...] = (a_ref[...].astype(F32) + b_ref[...].astype(F32)).astype(BF)


def pair_of(a, b, *after):
    block = pl.BlockSpec((224, 1024), lambda i: (i, 0))
    return pl.pallas_call(
        pair_kernel,
        grid=(4,),
        out_shape=jax.ShapeDtypeStruct((896, 1024), BF),
        in_specs=[block] * 2 + [ANY] * len(after),
        out_specs=block,
        compiler_params=PARAMS,
        cost_estimate=cost(2**20, 5),
        name="weight_sum",
    )(a, b, *after)


def ends_kernel(gate_ref, up_ref, here_ref, b_ref, c_ref, d_ref, e_ref, *refs):
    grad = here_ref[...].astype(F32) + b_ref[128:].astype(F32) + c_ref[...].astype(F32)
    grad = grad + (d_ref[...].astype(F32) + e_ref[...].astype(F32))
    g, u = gate_ref[...].astype(F32), up_ref[...].astype(F32)
    sig = jax.nn.sigmoid(g)
    refs[-2][...] = (grad * u * sig * (1.0 + g * (1.0 - sig))).astype(BF)
    refs[-1][...] = (grad * (g * sig)).astype(BF)


def ends_of(gate, up, here, b, c, d, e, *after):
    return pl.pallas_call(
        ends_kernel,
        out_shape=[jax.ShapeDtypeStruct((128, 896), BF)] * 2,
        in_specs=[VMEM] * 7 + [ANY] * len(after),
        out_specs=[VMEM] * 2,
        compiler_params=PARAMS,
        cost_estimate=cost(2**21, 2),
        name="gradients",
    )(gate, up, here, b, c, d, e, *after)


def sum_kernel(a_ref, b_ref, p2_ref, p1_ref, m1_ref, *refs):
    c, d, e = refs[-3:]
    c[...] = (a_ref[:128].astype(F32) + p2_ref[...].astype(F32)).astype(BF)
    d[...] = (a_ref[128:].astype(F32) + p1_ref[...].astype(F32)).astype(BF)
    e[...] = (b_ref[:128].astype(F32) + m1_ref[...].astype(F32)).astype(BF)


def sums_of(a, b, p2, p1, m1, *after):
    return pl.pallas_call(
        sum_kernel,
        out_shape=[jax.ShapeDtypeStruct((128, 896), BF)] * 3,
        in_specs=[VMEM] * 5 + [ANY] * len(after),
        out_specs=[VMEM] * 3,
        compiler_params=PARAMS,
        cost_estimate=cost(2**18, 1),
        name="sums",
    )(a, b, p2, p1, m1, *after)


def per_device(gate, up, w, cot):
    pos = jnp.stack([lax.axis_index(a) for a in AXES]).astype(jnp.int32)
    hid = lax.all_gather(hidden_of(gate, up), RING, axis=0, tiled=True)
    near = exchange(copies_of(pos, cot, False))
    rest = copies_of(pos, cot, True, near)
    p43, m32, p2, p1, m1, here = terms_of(pos, near, w, rest)
    rest = exchange(rest)

    right, left, right2, left2 = ring_move(1), ring_move(-1), ring_move(2), ring_move(-2)
    a, b = send(p43, right2), send(m32, left2)
    o = out_of(pos, hid, w)
    c, d, e = sums_of(a, b, p2, p1, m1)
    c, d, e = send(c, right2), send(d, right), send(e, left)
    output = total_of(exchange(o.reshape(16, 64, 1024)))
    grad_gate, grad_up = ends_of(gate, up, here, b, c, d, e, output)

    part = grad_of(pos, hid, near, rest, o, a, b)
    grad_weight = pair_of(part, send(part, SWAP_CORE))
    return output, grad_gate, grad_up, grad_weight


def solution(mesh):
    mesh = Mesh(mesh.devices.reshape(DIMS), AXES)
    depth = ("zhi", "core")
    by_col, by_row = P(depth + ("col",), PLANE), P(depth + PLANE, "col")
    weight = P(PLANE, "col")
    return jax.shard_map(
        per_device,
        mesh=mesh,
        in_specs=(by_col, by_col, weight, by_row),
        out_specs=(by_row, by_col, by_col, weight),
        check_vma=False,
    )
```

```python
import functools

import jax
import jax.numpy as jnp
from jax import lax
from jax.experimental import pallas as pl
from jax.experimental.pallas import tpu as pltpu
from jax.sharding import Mesh
from jax.sharding import PartitionSpec as P

BF, F32 = jnp.bfloat16, jnp.float32
AXES = ("zhi", "core", "x", "y", "col")
DIMS = (2, 2, 4, 4, 8)
RING = ("zhi", "col")
PLANE = ("x", "y")
VMEM_LIMIT = 20 * 2**20


def flat(c):
    n = 0
    for v, d in zip(c, DIMS):
        n = n * d + v % d
    return n


def pairs(move):
    out = []
    for h in range(2):
        for k in range(2):
            for x in range(4):
                for y in range(4):
                    for c in range(8):
                        out.append((flat((h, k, x, y, c)), flat(move(h, k, x, y, c))))
    return out


def ring_move(s):
    def move(h, k, x, y, c):
        z = (h * 8 + c + s) % 16
        return (z // 8, k, x, y, z % 8)

    return pairs(move)


def half_of(h0, col, row):
    k = (row // 2 - col + 11) % 8 - 3
    return (h0 * 8 + col + k + 16) % 16 // 8


def swap_z(wanted):
    out = []
    for h in range(2):
        for k in range(2):
            for x in range(4):
                for y in range(4):
                    for c in range(8):
                        if (half_of(h, c, x * 4 + y) == h) == wanted:
                            out.append((flat((h, k, x, y, c)), flat((1 - h, k, x, y, c))))
    return out


SWAP_CORE = pairs(lambda h, k, x, y, c: (h, 1 - k, x, y, c))
SMEM = pl.BlockSpec(memory_space=pltpu.SMEM)
VMEM = pl.BlockSpec(memory_space=pltpu.VMEM)
ANY = pl.BlockSpec(memory_space=pl.ANY)
PARAMS = pltpu.CompilerParams(vmem_limit_bytes=VMEM_LIMIT)
ALONE = pltpu.CompilerParams(vmem_limit_bytes=60 * 2**20)


def cost(flops, mib):
    return pl.CostEstimate(flops=flops, bytes_accessed=int(mib * 2**20), transcendentals=0)


def send(a, perm):
    return lax.ppermute(a, AXES, perm)


def started(moves):
    for m in moves:
        m.start()
    return moves


def hidden_kernel(gate_ref, up_ref, out_ref, g_ref, u_ref, sems):
    moves = started(
        [
            pltpu.make_async_copy(src.at[pl.ds(64 * i, 64)], dst.at[pl.ds(64 * i, 64)], sems.at[2 * i + n])
            for i in range(2)
            for n, (src, dst) in enumerate(((gate_ref, g_ref), (up_ref, u_ref)))
        ]
    )
    for i in range(2):
        moves[2 * i].wait()
        moves[2 * i + 1].wait()
        s = slice(64 * i, 64 * i + 64)
        g = g_ref[s].astype(F32)
        out_ref[s] = (g * jax.nn.sigmoid(g) * u_ref[s].astype(F32)).astype(BF)


def hidden_of(gate, up):
    return pl.pallas_call(
        hidden_kernel,
        out_shape=jax.ShapeDtypeStruct(gate.shape, BF),
        in_specs=[ANY, ANY],
        out_specs=VMEM,
        scratch_shapes=[pltpu.VMEM((128, 896), BF), pltpu.VMEM((128, 896), BF), pltpu.SemaphoreType.DMA((4,))],
        compiler_params=ALONE,
        cost_estimate=cost(2**20, 1),
        name="hidden",
    )(gate, up)


def copies_kernel(far_wanted, pos_ref, cot_ref, far_ref, *refs):
    mine = half_of(pos_ref[0], pos_ref[4], pos_ref[2] * 4 + pos_ref[3]) == pos_ref[0]

    def fill(ref):
        for i in range(16):
            refs[-1][i] = ref[...]

    pl.when(mine if far_wanted else jnp.logical_not(mine))(lambda: fill(far_ref))
    pl.when(jnp.logical_not(mine) if far_wanted else mine)(lambda: fill(cot_ref))


def copies_of(pos, cot, far_wanted, *after):
    return pl.pallas_call(
        functools.partial(copies_kernel, far_wanted),
        out_shape=jax.ShapeDtypeStruct((16, 64, 1024), BF),
        in_specs=[SMEM, VMEM, VMEM] + [ANY] * len(after),
        out_specs=VMEM,
        compiler_params=PARAMS,
        cost_estimate=cost(0, 2),
        name="copies",
    )(pos, cot, send(cot, swap_z(far_wanted)), *after)


def exchange(blocks):
    return lax.all_to_all(blocks, PLANE, 0, 0, tiled=True)


def term_kernel(parts, pos_ref, near_ref, w_ref, *refs):
    outs = refs[len(refs) - len(parts) :]
    for part, out in zip(parts, outs):
        rows = [near_ref[(pos_ref[4] + k + 8) % 8] for k in part]
        out[...] = lax.dot_general(
            rows[0] if len(rows) == 1 else jnp.concatenate(rows, axis=0),
            w_ref[...],
            (((1,), (1,)), ((), ())),
            preferred_element_type=F32,
        ).astype(BF)


def terms_of(parts, pos, near, w, *after):
    n = sum(len(p) for p in parts)
    return pl.pallas_call(
        functools.partial(term_kernel, parts),
        out_shape=[jax.ShapeDtypeStruct((128 * len(p), 896), BF) for p in parts],
        in_specs=[SMEM, VMEM, VMEM] + [ANY] * len(after),
        out_specs=[VMEM] * len(parts),
        compiler_params=PARAMS,
        cost_estimate=cost(2 * 128 * n * 896 * 1024, 4),
        name="hidden_terms",
    )(pos, near.reshape(8, 128, 1024), w, *after)


def out_kernel(pos_ref, hid_ref, w_ref, out_ref):
    at = pos_ref[0] * 1024
    for i in range(4):
        a = hid_ref[pl.ds(pl.multiple_of(at + 256 * i, 256), 256), :]
        out_ref[256 * i : 256 * i + 256] = jnp.dot(a, w_ref[...], preferred_element_type=F32).astype(BF)


def out_of(pos, hid, w):
    return pl.pallas_call(
        out_kernel,
        out_shape=jax.ShapeDtypeStruct((1024, 1024), BF),
        in_specs=[SMEM, VMEM, VMEM],
        out_specs=VMEM,
        compiler_params=PARAMS,
        cost_estimate=cost(2 * 1024 * 896 * 1024, 8),
        name="output_terms",
    )(pos, hid, w)


def total_kernel(got_ref, out_ref):
    total = got_ref[0].astype(F32)
    for i in range(1, 16):
        total = total + got_ref[i].astype(F32)
    out_ref[...] = total.astype(BF)


def total_of(got):
    return pl.pallas_call(
        total_kernel,
        grid=(4,),
        out_shape=jax.ShapeDtypeStruct((64, 1024), BF),
        in_specs=[pl.BlockSpec((16, 16, 1024), lambda i: (0, i, 0))],
        out_specs=pl.BlockSpec((16, 1024), lambda i: (i, 0)),
        compiler_params=PARAMS,
        cost_estimate=cost(2**20, 2),
        name="output_sum",
    )(got)


def grad_kernel(pos_ref, hid_ref, near_ref, rest_ref, *refs):
    out_ref, cot_ref = refs[-2:]
    h0, col = pos_ref[0], pos_ref[4]

    @pl.when(pl.program_id(0) == 0)
    def _():
        for r in range(16):
            h = half_of(h0, col, r)
            cot_ref[pl.ds(pl.multiple_of(h * 1024 + r * 64, 64), 64), :] = near_ref[r]
            cot_ref[pl.ds(pl.multiple_of((1 - h) * 1024 + r * 64, 64), 64), :] = rest_ref[r]

    n = pl.multiple_of(pl.program_id(0) * 256, 256)
    out_ref[...] = lax.dot_general(
        hid_ref[...], cot_ref[:, pl.ds(n, 256)], (((0,), (0,)), ((), ())), preferred_element_type=F32
    ).astype(BF)


def grad_of(pos, hid, near, rest, *after):
    return pl.pallas_call(
        grad_kernel,
        grid=(4,),
        out_shape=jax.ShapeDtypeStruct((896, 1024), BF),
        in_specs=[SMEM, VMEM, VMEM, VMEM] + [ANY] * len(after),
        out_specs=pl.BlockSpec((896, 256), lambda n: (0, n)),
        scratch_shapes=[pltpu.VMEM((2048, 1024), BF)],
        compiler_params=PARAMS,
        cost_estimate=cost(2 * 2048 * 896 * 1024, 10),
        name="weight_terms",
    )(pos, hid, near, rest, *after)


def pair_kernel(a_ref, b_ref, *refs):
    refs[-1][...] = (a_ref[...].astype(F32) + b_ref[...].astype(F32)).astype(BF)


def pair_of(a, b, *after):
    block = pl.BlockSpec((224, 1024), lambda i: (i, 0))
    return pl.pallas_call(
        pair_kernel,
        grid=(4,),
        out_shape=jax.ShapeDtypeStruct((896, 1024), BF),
        in_specs=[block] * 2 + [ANY] * len(after),
        out_specs=block,
        compiler_params=PARAMS,
        cost_estimate=cost(2**20, 5),
        name="weight_sum",
    )(a, b, *after)


def ends_kernel(gate_ref, up_ref, here_ref, a_ref, b_ref, *refs):
    grad = here_ref[...].astype(F32) + a_ref[...].astype(F32) + b_ref[...].astype(F32)
    g, u = gate_ref[...].astype(F32), up_ref[...].astype(F32)
    sig = jax.nn.sigmoid(g)
    refs[-2][...] = (grad * u * sig * (1.0 + g * (1.0 - sig))).astype(BF)
    refs[-1][...] = (grad * (g * sig)).astype(BF)


def ends_of(gate, up, here, a, b, *after):
    return pl.pallas_call(
        ends_kernel,
        out_shape=[jax.ShapeDtypeStruct((128, 896), BF)] * 2,
        in_specs=[VMEM] * 5 + [ANY] * len(after),
        out_specs=[VMEM] * 2,
        compiler_params=PARAMS,
        cost_estimate=cost(2**21, 2),
        name="gradients",
    )(gate, up, here, a, b, *after)


def add_kernel(n, *refs):
    outs = refs[len(refs) - n :]
    for i in range(n):
        outs[i][...] = (refs[2 * i][...].astype(F32) + refs[2 * i + 1][...].astype(F32)).astype(BF)


def add(pairs_of, *after):
    out = pl.pallas_call(
        functools.partial(add_kernel, len(pairs_of)),
        out_shape=[jax.ShapeDtypeStruct((128, 896), BF)] * len(pairs_of),
        in_specs=[VMEM] * (2 * len(pairs_of)) + [ANY] * len(after),
        out_specs=[VMEM] * len(pairs_of),
        compiler_params=PARAMS,
        cost_estimate=cost(2**18, 1),
        name="sums",
    )(*[v for p in pairs_of for v in p], *after)
    return out


def per_device(gate, up, w, cot):
    pos = jnp.stack([lax.axis_index(a) for a in AXES]).astype(jnp.int32)
    hid = lax.all_gather(hidden_of(gate, up), RING, axis=0, tiled=True)
    near = exchange(copies_of(pos, cot, False))
    rest = copies_of(pos, cot, True, near)
    parts = ((4,), (-3,), (3,), (-2,), (2,), (-1,), (1,), (0,))
    p4, m3, p3, m2, p2, m1, p1, here = terms_of(parts, pos, near, w, rest)
    rest = exchange(rest)

    right, left = ring_move(1), ring_move(-1)
    o = out_of(pos, hid, w)
    a1, b1 = send(p4, right), send(m3, left)
    a, b = add(((a1, p3), (b1, m2)))
    a2, b2 = send(a, right), send(b, left)
    a, b = add(((a2, p2), (b2, m1)))
    a3, b = send(a, right), send(b, left)
    (a,) = add(((a3, p1),), o)
    a = send(a, right)
    output = total_of(exchange(o.reshape(16, 64, 1024)))
    grad_gate, grad_up = ends_of(gate, up, here, a, b, output)

    part = grad_of(pos, hid, near, rest, o, a3, b)
    grad_weight = pair_of(part, send(part, SWAP_CORE))
    return output, grad_gate, grad_up, grad_weight


def solution(mesh):
    mesh = Mesh(mesh.devices.reshape(DIMS), AXES)
    depth = ("zhi", "core")
    by_col, by_row = P(depth + ("col",), PLANE), P(depth + PLANE, "col")
    weight = P(PLANE, "col")
    return jax.shard_map(
        per_device,
        mesh=mesh,
        in_specs=(by_col, by_col, weight, by_row),
        out_specs=(by_row, by_col, by_col, weight),
        check_vma=False,
    )
```

```python
import functools

import jax
import jax.numpy as jnp
from jax import lax
from jax.experimental import pallas as pl
from jax.experimental.pallas import tpu as pltpu
from jax.sharding import Mesh
from jax.sharding import PartitionSpec as P

BF, F32 = jnp.bfloat16, jnp.float32
AXES = ("zhi", "core", "x", "y", "col")
DIMS = (2, 2, 4, 4, 8)
RING = ("zhi", "col")
PLANE = ("x", "y")
VMEM_LIMIT = 20 * 2**20


def flat(c):
    n = 0
    for v, d in zip(c, DIMS):
        n = n * d + v % d
    return n


def pairs(move):
    out = []
    for h in range(2):
        for k in range(2):
            for x in range(4):
                for y in range(4):
                    for c in range(8):
                        out.append((flat((h, k, x, y, c)), flat(move(h, k, x, y, c))))
    return out


def ring_move(s):
    def move(h, k, x, y, c):
        z = (h * 8 + c + s) % 16
        return (z // 8, k, x, y, z % 8)

    return pairs(move)


def half_of(h0, col, row):
    k = (row // 2 - col + 11) % 8 - 3
    return (h0 * 8 + col + k + 16) % 16 // 8


def swap_z(wanted):
    out = []
    for h in range(2):
        for k in range(2):
            for x in range(4):
                for y in range(4):
                    for c in range(8):
                        if (half_of(h, c, x * 4 + y) == h) == wanted:
                            out.append((flat((h, k, x, y, c)), flat((1 - h, k, x, y, c))))
    return out


SWAP_CORE = pairs(lambda h, k, x, y, c: (h, 1 - k, x, y, c))
SMEM = pl.BlockSpec(memory_space=pltpu.SMEM)
VMEM = pl.BlockSpec(memory_space=pltpu.VMEM)
ANY = pl.BlockSpec(memory_space=pl.ANY)
PARAMS = pltpu.CompilerParams(vmem_limit_bytes=VMEM_LIMIT)
ALONE = pltpu.CompilerParams(vmem_limit_bytes=60 * 2**20)


def cost(flops, mib):
    return pl.CostEstimate(flops=flops, bytes_accessed=int(mib * 2**20), transcendentals=0)


def send(a, perm):
    return lax.ppermute(a, AXES, perm)


def started(moves):
    for m in moves:
        m.start()
    return moves


def hidden_kernel(gate_ref, up_ref, out_ref, g_ref, u_ref, sems):
    moves = started(
        [
            pltpu.make_async_copy(src.at[pl.ds(64 * i, 64)], dst.at[pl.ds(64 * i, 64)], sems.at[2 * i + n])
            for i in range(2)
            for n, (src, dst) in enumerate(((gate_ref, g_ref), (up_ref, u_ref)))
        ]
    )
    for i in range(2):
        moves[2 * i].wait()
        moves[2 * i + 1].wait()
        s = slice(64 * i, 64 * i + 64)
        g = g_ref[s].astype(F32)
        out_ref[s] = (g * jax.nn.sigmoid(g) * u_ref[s].astype(F32)).astype(BF)


def hidden_of(gate, up):
    return pl.pallas_call(
        hidden_kernel,
        out_shape=jax.ShapeDtypeStruct(gate.shape, BF),
        in_specs=[ANY, ANY],
        out_specs=VMEM,
        scratch_shapes=[pltpu.VMEM((128, 896), BF), pltpu.VMEM((128, 896), BF), pltpu.SemaphoreType.DMA((4,))],
        compiler_params=ALONE,
        cost_estimate=cost(2**20, 1),
        name="hidden",
    )(gate, up)


def copies_kernel(far_wanted, pos_ref, cot_ref, far_ref, *refs):
    mine = half_of(pos_ref[0], pos_ref[4], pos_ref[2] * 4 + pos_ref[3]) == pos_ref[0]

    def fill(ref):
        for i in range(16):
            refs[-1][i] = ref[...]

    pl.when(mine if far_wanted else jnp.logical_not(mine))(lambda: fill(far_ref))
    pl.when(jnp.logical_not(mine) if far_wanted else mine)(lambda: fill(cot_ref))


def copies_of(pos, cot, far_wanted, *after):
    return pl.pallas_call(
        functools.partial(copies_kernel, far_wanted),
        out_shape=jax.ShapeDtypeStruct((16, 64, 1024), BF),
        in_specs=[SMEM, VMEM, VMEM] + [ANY] * len(after),
        out_specs=VMEM,
        compiler_params=PARAMS,
        cost_estimate=cost(0, 2),
        name="copies",
    )(pos, cot, send(cot, swap_z(far_wanted)), *after)


def exchange(blocks):
    return lax.all_to_all(blocks, PLANE, 0, 0, tiled=True)


def term_kernel(parts, pos_ref, near_ref, w_ref, *refs):
    outs = refs[len(refs) - len(parts) :]
    for part, out in zip(parts, outs):
        rows = [near_ref[(pos_ref[4] + k + 8) % 8] for k in part]
        out[...] = lax.dot_general(
            rows[0] if len(rows) == 1 else jnp.concatenate(rows, axis=0),
            w_ref[...],
            (((1,), (1,)), ((), ())),
            preferred_element_type=F32,
        ).astype(BF)


def terms_of(parts, pos, near, w, *after):
    n = sum(len(p) for p in parts)
    return pl.pallas_call(
        functools.partial(term_kernel, parts),
        out_shape=[jax.ShapeDtypeStruct((128 * len(p), 896), BF) for p in parts],
        in_specs=[SMEM, VMEM, VMEM] + [ANY] * len(after),
        out_specs=[VMEM] * len(parts),
        compiler_params=PARAMS,
        cost_estimate=cost(2 * 128 * n * 896 * 1024, 4),
        name="hidden_terms",
    )(pos, near.reshape(8, 128, 1024), w, *after)


def out_kernel(pos_ref, hid_ref, w_ref, out_ref):
    at = pos_ref[0] * 1024
    for i in range(4):
        a = hid_ref[pl.ds(pl.multiple_of(at + 256 * i, 256), 256), :]
        out_ref[256 * i : 256 * i + 256] = jnp.dot(a, w_ref[...], preferred_element_type=F32).astype(BF)


def out_of(pos, hid, w):
    return pl.pallas_call(
        out_kernel,
        out_shape=jax.ShapeDtypeStruct((1024, 1024), BF),
        in_specs=[SMEM, VMEM, VMEM],
        out_specs=VMEM,
        compiler_params=PARAMS,
        cost_estimate=cost(2 * 1024 * 896 * 1024, 8),
        name="output_terms",
    )(pos, hid, w)


def total_kernel(got_ref, out_ref):
    total = got_ref[0].astype(F32)
    for i in range(1, 16):
        total = total + got_ref[i].astype(F32)
    out_ref[...] = total.astype(BF)


def total_of(got):
    return pl.pallas_call(
        total_kernel,
        grid=(4,),
        out_shape=jax.ShapeDtypeStruct((64, 1024), BF),
        in_specs=[pl.BlockSpec((16, 16, 1024), lambda i: (0, i, 0))],
        out_specs=pl.BlockSpec((16, 1024), lambda i: (i, 0)),
        compiler_params=PARAMS,
        cost_estimate=cost(2**20, 2),
        name="output_sum",
    )(got)


def grad_kernel(pos_ref, hid_ref, near_ref, rest_ref, *refs):
    out_ref, cot_ref = refs[-2:]
    h0, col = pos_ref[0], pos_ref[4]

    @pl.when(pl.program_id(0) == 0)
    def _():
        for r in range(16):
            h = half_of(h0, col, r)
            cot_ref[pl.ds(pl.multiple_of(h * 1024 + r * 64, 64), 64), :] = near_ref[r]
            cot_ref[pl.ds(pl.multiple_of((1 - h) * 1024 + r * 64, 64), 64), :] = rest_ref[r]

    n = pl.multiple_of(pl.program_id(0) * 256, 256)
    out_ref[...] = lax.dot_general(
        hid_ref[...], cot_ref[:, pl.ds(n, 256)], (((0,), (0,)), ((), ())), preferred_element_type=F32
    ).astype(BF)


def grad_of(pos, hid, near, rest, *after):
    return pl.pallas_call(
        grad_kernel,
        grid=(4,),
        out_shape=jax.ShapeDtypeStruct((896, 1024), BF),
        in_specs=[SMEM, VMEM, VMEM, VMEM] + [ANY] * len(after),
        out_specs=pl.BlockSpec((896, 256), lambda n: (0, n)),
        scratch_shapes=[pltpu.VMEM((2048, 1024), BF)],
        compiler_params=PARAMS,
        cost_estimate=cost(2 * 2048 * 896 * 1024, 10),
        name="weight_terms",
    )(pos, hid, near, rest, *after)


def pair_kernel(a_ref, b_ref, *refs):
    refs[-1][...] = (a_ref[...].astype(F32) + b_ref[...].astype(F32)).astype(BF)


def pair_of(a, b, *after):
    block = pl.BlockSpec((224, 1024), lambda i: (i, 0))
    return pl.pallas_call(
        pair_kernel,
        grid=(4,),
        out_shape=jax.ShapeDtypeStruct((896, 1024), BF),
        in_specs=[block] * 2 + [ANY] * len(after),
        out_specs=block,
        compiler_params=PARAMS,
        cost_estimate=cost(2**20, 5),
        name="weight_sum",
    )(a, b, *after)


def ends_kernel(gate_ref, up_ref, here_ref, a_ref, b_ref, *refs):
    grad = here_ref[...].astype(F32) + a_ref[...].astype(F32) + b_ref[...].astype(F32)
    g, u = gate_ref[...].astype(F32), up_ref[...].astype(F32)
    sig = jax.nn.sigmoid(g)
    refs[-2][...] = (grad * u * sig * (1.0 + g * (1.0 - sig))).astype(BF)
    refs[-1][...] = (grad * (g * sig)).astype(BF)


def ends_of(gate, up, here, a, b, *after):
    return pl.pallas_call(
        ends_kernel,
        out_shape=[jax.ShapeDtypeStruct((128, 896), BF)] * 2,
        in_specs=[VMEM] * 5 + [ANY] * len(after),
        out_specs=[VMEM] * 2,
        compiler_params=PARAMS,
        cost_estimate=cost(2**21, 2),
        name="gradients",
    )(gate, up, here, a, b, *after)


def add_kernel(n, *refs):
    outs = refs[len(refs) - n :]
    for i in range(n):
        outs[i][...] = (refs[2 * i][...].astype(F32) + refs[2 * i + 1][...].astype(F32)).astype(BF)


def add(pairs_of, *after):
    out = pl.pallas_call(
        functools.partial(add_kernel, len(pairs_of)),
        out_shape=[jax.ShapeDtypeStruct((128, 896), BF)] * len(pairs_of),
        in_specs=[VMEM] * (2 * len(pairs_of)) + [ANY] * len(after),
        out_specs=[VMEM] * len(pairs_of),
        compiler_params=PARAMS,
        cost_estimate=cost(2**18, 1),
        name="sums",
    )(*[v for p in pairs_of for v in p], *after)
    return out


def per_device(gate, up, w, cot):
    pos = jnp.stack([lax.axis_index(a) for a in AXES]).astype(jnp.int32)
    hid = lax.all_gather(hidden_of(gate, up), RING, axis=0, tiled=True)
    near = exchange(copies_of(pos, cot, False))
    rest = copies_of(pos, cot, True, near)
    parts = ((4,), (-3,), (3,), (-2,), (2,), (-1,), (1,), (0,))
    p4, m3, p3, m2, p2, m1, p1, here = terms_of(parts, pos, near, w, rest)
    rest = exchange(rest)

    right, left = ring_move(1), ring_move(-1)
    o = out_of(pos, hid, w)
    a1, b1 = send(p4, right), send(m3, left)
    a, b = add(((a1, p3), (b1, m2)))
    a2, b2 = send(a, right), send(b, left)
    a, b = add(((a2, p2), (b2, m1)))
    a3, b = send(a, right), send(b, left)
    (a,) = add(((a3, p1),))
    a = send(a, right)
    output = total_of(exchange(o.reshape(16, 64, 1024)))
    grad_gate, grad_up = ends_of(gate, up, here, a, b, output)

    part = grad_of(pos, hid, near, rest, o, a2, b2)
    grad_weight = pair_of(part, send(part, SWAP_CORE))
    return output, grad_gate, grad_up, grad_weight


def solution(mesh):
    mesh = Mesh(mesh.devices.reshape(DIMS), AXES)
    depth = ("zhi", "core")
    by_col, by_row = P(depth + ("col",), PLANE), P(depth + PLANE, "col")
    weight = P(PLANE, "col")
    return jax.shard_map(
        per_device,
        mesh=mesh,
        in_specs=(by_col, by_col, weight, by_row),
        out_specs=(by_row, by_col, by_col, weight),
        check_vma=False,
    )
```
